32 devices in a mesh: fsdp: 8 (over y, x, core), grp: 4 (over z).
Axes of the slice: x: 2, y: 2, z: 4, core: 2. Of those that a mesh axis runs over, the one named last changes fastest.
Arguments:
- q_up: bfloat16 [128, 128, 1536], P('grp', None, 'fsdp'), may hold values from -0.15625 to 0.15625
- k_up: bfloat16 [128, 128, 512], P('grp', None, 'fsdp'), may hold values from -0.25 to 0.25
- v_up: bfloat16 [128, 128, 512], P('grp', None, 'fsdp'), may hold values from -0.25 to 0.25
- queries: bfloat16 [512, 1536], P(('fsdp', 'grp')), may hold values from -6 to 6
- cache: bfloat16 [65536, 512], P(('fsdp', 'grp')), may hold values from -360 to 360
- positions: int32 [512], P(('fsdp', 'grp')), may hold values from 256 to 2047, as said below
Outputs:
- heads_out: bfloat16 [512, 16384], P(('fsdp', 'grp'))
The draws below stay inside these ranges and needn't reach their ends.
Inputs may be any that keep to these rules, and one draw needn't show every extreme that they name: `positions`: each row reads its own device's cache block up to this entry; some row reads the whole block.
All inputs are finite; a program needn't handle non-finite values.
Results may differ from the reference program's by a relative error of at most 0.006.
The reference program's roundings to bfloat16 on the way count: a program that leaves them out, or rounds other values in their place, can miss the bound.
Values may be sent and summed in bfloat16 or wider, within the bound.
A program may use at most 128 MiB of HBM per device.

```python
import jax
import jax.numpy as jnp
from jax import lax

HEADS = 128
HD = 128
QR = 1536
KR = 512
ROWS_DEV = 16
CACHE = 2048
ROWS = 512
CACHE_ALL = 65536
N_FSDP = 8
N_GRP = 4


def draw_positions(key, part):
    key = jax.random.fold_in(key, 11)
    first_key, second_key = jax.random.split(key)
    values = jax.random.randint(first_key, (ROWS,), CACHE // 8, CACHE)
    chosen = jax.random.randint(second_key, (), 0, ROWS)
    return values.at[chosen].set(CACHE - 1).astype(jnp.int32)


def draw_cache(key, part):
    key = jax.random.fold_in(key, 23)
    base_key = jax.random.fold_in(key, 0)
    values = jax.random.truncated_normal(base_key, -6.0, 6.0, (CACHE_ALL, KR), jnp.float32)
    return values.astype(jnp.bfloat16)


def block_levels(rng, dims, cuts, least, top_value):
    level, own = 1.0, jax.random.fold_in(rng, 6)
    for position, blocks in cuts:
        heights = jnp.exp(jax.random.uniform(jax.random.fold_in(own, position), (blocks,), jnp.float32, least / len(cuts), top_value / len(cuts)))
        level = level * jnp.repeat(heights, dims[position] // blocks).reshape([-1 if axis == position else 1 for axis in range(len(dims))])
    return level


def normal_values(key, dims, width, reach, shards=(), held_as=jnp.bfloat16):
    entries = jax.random.normal(key, dims, jnp.float32) * width
    if len(shards) > 0:
        entries = block_levels(key, dims, shards, -0.22, 0.18) * entries
    return jnp.clip(entries, min=-reach, max=reach).astype(held_as)


def setup_inputs(seed: int = 0) -> dict:
    splits = jax.random.split(jax.random.key(seed), 7)
    q_up = normal_values(splits[0], (HEADS, HD, QR), QR ** -0.5, 0.15625, ((0, 4), (2, 8)))
    k_up = normal_values(splits[1], (HEADS, HD, KR), KR ** -0.5, 0.25, ((0, 4), (2, 8)))
    v_up = normal_values(splits[2], (HEADS, HD, KR), KR ** -0.5, 0.25, ((0, 4), (2, 8)))
    queries = normal_values(splits[3], (ROWS, QR), 1.0, 6.0, ((0, 32),))
    cache = draw_cache(jax.random.fold_in(splits[6], 71), 0)
    positions = draw_positions(jax.random.fold_in(splits[6], 71), 0)
    return {"q_up": q_up, "k_up": k_up, "v_up": v_up, "queries": queries, "cache": cache, "positions": positions}


score_scale = 192.0 ** -0.5


def attend(q_abs, keys, row_pos):
    scores = jnp.einsum('rhk,jk->rhj', q_abs.astype(jnp.float32), keys.astype(jnp.float32)) * score_scale
    cache_index = jnp.arange(keys.shape[0], dtype=jnp.int32)
    visible = cache_index[None, :] <= row_pos[:, None]
    scores = jnp.where(visible[:, None, :], scores, jnp.float32(-1e30))
    row_max = jnp.max(scores, axis=-1, keepdims=True)
    weights = jnp.exp(scores - row_max)
    attention = (weights / jnp.sum(weights, axis=-1, keepdims=True)).astype(jnp.bfloat16)
    latent = jnp.einsum('rhj,jk->rhk', attention.astype(jnp.float32), keys.astype(jnp.float32))
    return latent.astype(jnp.bfloat16)


def reference(q_up, k_up, v_up, queries, cache, positions):
    absorbed = jnp.einsum('hdq,hdk->hqk', q_up.astype(jnp.float32), k_up.astype(jnp.float32)).astype(jnp.bfloat16)
    flat_blocks = jnp.transpose(absorbed, (1, 0, 2)).reshape(QR, HEADS * KR)
    q_abs = jnp.dot(queries, flat_blocks, preferred_element_type=jnp.float32).astype(jnp.bfloat16)
    device_count = N_FSDP * N_GRP
    q_groups = q_abs.reshape(device_count, ROWS_DEV, HEADS, KR)
    key_groups = cache.reshape(device_count, CACHE, KR)
    pos_groups = positions.reshape(device_count, ROWS_DEV)
    value_proj = v_up.astype(jnp.float32)

    def one_device(device_data):
        row_queries, key_data, row_pos = device_data
        latent = attend(row_queries, key_data, row_pos)
        projected = jnp.einsum('rhk,hdk->rhd', latent.astype(jnp.float32), value_proj)
        return projected.astype(jnp.bfloat16).reshape(ROWS_DEV, HEADS * HD)

    result = lax.map(one_device, (q_groups, key_groups, pos_groups))
    return result.reshape(ROWS, HEADS * HD)
```

```python
import functools

import jax
import jax.numpy as jnp
from jax import lax
from jax.experimental import pallas as pl
from jax.experimental.pallas import tpu as pltpu
from jax.sharding import PartitionSpec as P

score_scale = 192.0 ** (-0.5)
ROW_BLOCK = 2


def attend_body(pos_ref, q_ref, cache_ref, out_ref):
    step = pl.program_id(0)
    rows, heads, rank = q_ref.shape
    entries = cache_ref.shape[0]
    index = lax.broadcasted_iota(jnp.int32, (heads, entries), 1)
    for r in range(rows):
        scores = lax.dot_general(
            q_ref[r],
            cache_ref[...],
            (((1,), (1,)), ((), ())),
            preferred_element_type=jnp.float32,
        )
        scores = scores * score_scale
        scores = jnp.where(index <= pos_ref[step * rows + r], scores, jnp.float32(-1e30))
        top = jnp.max(scores, axis=-1, keepdims=True)
        weights = jnp.exp(scores - top)
        total = jnp.sum(weights, axis=-1, keepdims=True)
        probs = (weights * (1.0 / total)).astype(jnp.bfloat16)
        out_ref[r] = jnp.dot(
            probs, cache_ref[...], preferred_element_type=jnp.float32
        ).astype(jnp.bfloat16)


def attend(q_abs, keys, row_pos):
    rows, heads, rank = q_abs.shape
    block = ROW_BLOCK if rows % ROW_BLOCK == 0 else 1
    spec = pl.BlockSpec((block, heads, rank), lambda i, pos: (i, 0, 0))
    return pl.pallas_call(
        attend_body,
        out_shape=jax.ShapeDtypeStruct(q_abs.shape, jnp.bfloat16),
        grid_spec=pltpu.PrefetchScalarGridSpec(
            num_scalar_prefetch=1,
            grid=(rows // block,),
            in_specs=[spec, pl.BlockSpec(keys.shape, lambda i, pos: (0, 0))],
            out_specs=spec,
        ),
        compiler_params=pltpu.CompilerParams(vmem_limit_bytes=40 << 20),
        cost_estimate=pl.CostEstimate(
            flops=4 * rows * heads * keys.shape[0] * rank,
            bytes_accessed=2 * (2 * q_abs.size + keys.size),
            transcendentals=rows * heads * keys.shape[0],
        ),
    )(row_pos, q_abs, keys)


def absorb_heads(query_rows, key_rows):
    return jnp.einsum(
        "hdq,hdk->hqk", query_rows, key_rows, preferred_element_type=jnp.float32
    ).astype(jnp.bfloat16)


def shards(n_fsdp, n_grp, q_up, k_up, v_up, queries, cache, positions):
    rows = queries.shape[0]
    all_rows = lax.all_gather(queries, ("fsdp", "grp"), axis=0, tiled=True)
    own_query, own_key = (
        lax.all_to_all(q_up, "fsdp", split_axis=0, concat_axis=2, tiled=True),
        lax.all_to_all(k_up, "fsdp", split_axis=0, concat_axis=2, tiled=True),
    )
    own_blocks = absorb_heads(own_query, own_key)
    own_heads, _, rank = own_blocks.shape
    q_abs = jnp.einsum(
        "rq,hqk->rhk", all_rows, own_blocks, preferred_element_type=jnp.float32
    ).astype(jnp.bfloat16)
    row_queries = lax.all_to_all(
        q_abs, ("fsdp", "grp"), split_axis=0, concat_axis=1, tiled=True
    )
    latent = attend(row_queries, cache, positions)
    value_proj = lax.all_gather(v_up, "fsdp", axis=2, tiled=True)
    latent = latent.reshape(rows, n_fsdp, n_grp, own_heads * rank)
    by_heads = lax.all_to_all(latent, "grp", split_axis=2, concat_axis=0, tiled=True)
    by_heads = by_heads.reshape(rows * n_grp, n_fsdp * own_heads, rank)
    projected = jnp.einsum(
        "rhk,hdk->rhd", by_heads, value_proj, preferred_element_type=jnp.float32
    ).astype(jnp.bfloat16)
    result = lax.all_to_all(projected, "grp", split_axis=0, concat_axis=1, tiled=True)
    return result.reshape(result.shape[0], result.shape[1] * result.shape[2])


def solution(mesh):
    placed = (
        P("grp", None, "fsdp"),
        P("grp", None, "fsdp"),
        P("grp", None, "fsdp"),
        P(("fsdp", "grp"), None),
        P(("fsdp", "grp"), None),
        P(("fsdp", "grp")),
    )
    return jax.shard_map(
        functools.partial(shards, mesh.shape["fsdp"], mesh.shape["grp"]),
        mesh=mesh,
        in_specs=placed,
        out_specs=P(("fsdp", "grp"), None),
        check_vma=False,
    )
```

```python
import functools

import jax
import jax.numpy as jnp
from jax import lax
from jax.experimental import pallas as pl
from jax.experimental.pallas import tpu as pltpu
from jax.sharding import PartitionSpec as P

score_scale = 192.0 ** (-0.5)
VMEM = 50 << 20


def front_body(
    n_fsdp,
    n_grp,
    q_cols,
    qk_ref,
    queries_ref,
    out_ref,
    qk_all,
    rows_all,
    absorbed,
    local_sem,
    qk_send,
    qk_recv,
    grp_send,
    grp_recv,
    far_send,
    far_recv,
    pair_send,
    pair_recv,
):
    f, g = lax.axis_index("fsdp"), lax.axis_index("grp")
    pairs = n_fsdp // 2
    chip, core = lax.div(f, 2), lax.rem(f, 2)
    partner = chip * 2 + 1 - core

    def send(src, dst, sems, slot, target):
        return pltpu.make_async_remote_copy(
            src_ref=src,
            dst_ref=dst,
            send_sem=sems[0].at[target[2]],
            recv_sem=sems[1].at[slot],
            device_id=(target[0], target[1]),
            device_id_type=pl.DeviceIdType.MESH,
        )

    barrier = pltpu.get_barrier_semaphore()

    @pl.loop(1, n_fsdp)
    def _(step):
        pl.semaphore_signal(
            barrier,
            inc=1,
            device_id=(lax.rem(f + step, n_fsdp), g),
            device_id_type=pl.DeviceIdType.MESH,
        )

    @pl.loop(1, n_grp)
    def _(step):
        pl.semaphore_signal(
            barrier,
            inc=1,
            device_id=(f, lax.rem(g + step, n_grp)),
            device_id_type=pl.DeviceIdType.MESH,
        )

    own_qk = pltpu.make_async_copy(qk_ref.at[f], qk_all.at[f], local_sem.at[0])
    own_rows = pltpu.make_async_copy(queries_ref, rows_all.at[f, g], local_sem.at[1])
    own_qk.start()
    own_rows.start()
    pl.semaphore_wait(barrier, n_fsdp + n_grp - 2)

    def grp_copy(peer, slot):
        return send(
            queries_ref, rows_all.at[f, slot], (grp_send, grp_recv), slot, (f, peer, peer)
        )

    def qk_copy(peer, slot):
        return send(
            qk_ref.at[peer], qk_all.at[slot], (qk_send, qk_recv), slot, (peer, g, peer)
        )

    def far_copy(peer, slot):
        return send(
            rows_all.at[slot], rows_all.at[slot], (far_send, far_recv), slot, (peer, g, peer)
        )

    def pair_copy(slot):
        return send(
            rows_all.at[slot],
            rows_all.at[slot],
            (pair_send, pair_recv),
            lax.div(slot, 2),
            (partner, g, lax.div(slot, 2)),
        )

    @pl.loop(1, n_grp)
    def _(step):
        grp_copy(lax.rem(g + step, n_grp), g).start()

    @pl.loop(1, n_fsdp)
    def _(step):
        qk_copy(lax.rem(f + step, n_fsdp), f).start()

    own_rows.wait()

    @pl.loop(1, n_grp)
    def _(step):
        other = lax.rem(g + step, n_grp)
        grp_copy(other, other).wait_recv()

    @pl.loop(1, pairs)
    def _(step):
        far_copy(lax.rem(chip + step, pairs) * 2 + core, f).start()

    pair_copy(f).start()

    @pl.loop(1, pairs)
    def _(step):
        other = lax.rem(chip + step, pairs) * 2 + core
        far_copy(other, other).wait_recv()
        pair_copy(other).start()

    own_qk.wait()

    @pl.loop(1, n_fsdp)
    def _(step):
        other = lax.rem(f + step, n_fsdp)
        qk_copy(other, other).wait_recv()

    heads = qk_all.shape[1]

    @pl.loop(0, heads)
    def _(h):
        keys = jnp.concatenate([qk_all[s, h, :, q_cols:] for s in range(n_fsdp)], axis=-1)
        for s in range(n_fsdp):
            absorbed[h, s * q_cols : (s + 1) * q_cols, :] = lax.dot_general(
                qk_all[s, h, :, :q_cols],
                keys,
                (((0,), (0,)), ((), ())),
                preferred_element_type=jnp.float32,
            ).astype(jnp.bfloat16)

    @pl.loop(0, pairs)
    def _(step):
        pair_copy(step * 2 + 1 - core).wait_recv()

    devices, _, rows, rank = out_ref.shape

    @pl.loop(0, heads)
    def _(h):
        @pl.loop(0, n_fsdp)
        def _(s):
            block = rows_all[s].reshape(n_grp * rows, rows_all.shape[-1])
            q_abs = jnp.dot(block, absorbed[h], preferred_element_type=jnp.float32)
            out_ref[pl.ds(s * n_grp, n_grp), h] = q_abs.astype(jnp.bfloat16).reshape(
                n_grp, rows, rank
            )

    @pl.loop(1, n_grp)
    def _(step):
        grp_copy(lax.rem(g + step, n_grp), g).wait_send()

    @pl.loop(1, n_fsdp)
    def _(step):
        qk_copy(lax.rem(f + step, n_fsdp), f).wait_send()

    @pl.loop(1, pairs)
    def _(step):
        far_copy(lax.rem(chip + step, pairs) * 2 + core, f).wait_send()

    @pl.loop(0, pairs)
    def _(step):
        pair_copy(step * 2 + core).wait_send()


def absorbed_queries(n_fsdp, n_grp, qk, queries, q_cols):
    _, heads, hd, cols = qk.shape
    rows, q_rank = queries.shape
    rank = n_fsdp * (cols - q_cols)
    devices = n_fsdp * n_grp
    dma = pltpu.SemaphoreType.DMA
    return pl.pallas_call(
        functools.partial(front_body, n_fsdp, n_grp, q_cols),
        out_shape=jax.ShapeDtypeStruct((devices, heads, rows, rank), jnp.bfloat16),
        in_specs=[pl.BlockSpec(memory_space=pl.ANY)] * 2,
        out_specs=pl.BlockSpec(memory_space=pltpu.VMEM),
        scratch_shapes=[
            pltpu.VMEM((n_fsdp, heads, hd, cols), jnp.bfloat16),
            pltpu.VMEM((n_fsdp, n_grp, rows, q_rank), jnp.bfloat16),
            pltpu.VMEM((heads, q_rank, rank), jnp.bfloat16),
            dma((2,)),
            dma((n_fsdp,)),
            dma((n_fsdp,)),
            dma((n_grp,)),
            dma((n_grp,)),
            dma((n_fsdp,)),
            dma((n_fsdp,)),
            dma((n_fsdp // 2,)),
            dma((n_fsdp // 2,)),
        ],
        compiler_params=pltpu.CompilerParams(
            vmem_limit_bytes=VMEM, collective_id=0, has_side_effects=True
        ),
        cost_estimate=pl.CostEstimate(
            flops=2 * heads * q_rank * rank * (hd + rows * devices),
            bytes_accessed=2 * (qk.size + heads * rows * devices * rank),
            transcendentals=0,
        ),
    )(qk, queries)


def attend_body(pos_ref, q_ref, cache_ref, out_ref):
    block = q_ref.shape
    q = q_ref[...].reshape(-1, block[-1])
    entries = cache_ref.shape[0]
    index = lax.broadcasted_iota(jnp.int32, (q.shape[0], entries), 1)
    scores = lax.dot_general(
        q, cache_ref[...], (((1,), (1,)), ((), ())), preferred_element_type=jnp.float32
    )
    scores = jnp.where(index <= pos_ref[...], scores * score_scale, jnp.float32(-1e30))
    top = jnp.max(scores, axis=-1, keepdims=True)
    weights = jnp.exp(scores - top)
    total = jnp.sum(weights, axis=-1, keepdims=True)
    probs = (weights * (1.0 / total)).astype(jnp.bfloat16)
    latent = jnp.dot(probs, cache_ref[...], preferred_element_type=jnp.float32)
    out_ref[...] = latent.astype(jnp.bfloat16).reshape(block)


def attend(q_abs, keys, row_pos, per_step):
    devices, heads, rows, rank = q_abs.shape
    pos = jnp.tile(row_pos, per_step * heads)[:, None]
    spec = pl.BlockSpec((per_step, heads, rows, rank), lambda i: (i, 0, 0, 0))
    return pl.pallas_call(
        attend_body,
        out_shape=jax.ShapeDtypeStruct(q_abs.shape, jnp.bfloat16),
        grid=(devices // per_step,),
        in_specs=[
            pl.BlockSpec(pos.shape, lambda i: (0, 0)),
            spec,
            pl.BlockSpec(keys.shape, lambda i: (0, 0)),
        ],
        out_specs=spec,
        compiler_params=pltpu.CompilerParams(vmem_limit_bytes=VMEM),
        cost_estimate=pl.CostEstimate(
            flops=4 * q_abs.size * keys.shape[0],
            bytes_accessed=2 * (2 * q_abs.size + keys.size),
            transcendentals=q_abs.size // rank * keys.shape[0],
        ),
    )(pos, q_abs, keys)


def project_body(latent_ref, value_ref, out_ref):
    n_f, _, per, rows, rank = latent_ref.shape
    hd = value_ref.shape[-1]
    for f in range(n_f):
        for i in range(per):
            h = f * per + i
            out_ref[:, h * hd : (h + 1) * hd] = jnp.dot(
                latent_ref[f, 0, i],
                value_ref[:, 0, h].reshape(rank, hd),
                preferred_element_type=jnp.float32,
            ).astype(jnp.bfloat16)


def project(latent, values, f_step):
    n_f, n_g, per, rows, rank = latent.shape
    _, _, heads, cols, hd = values.shape
    steps = n_f // f_step
    return pl.pallas_call(
        project_body,
        out_shape=jax.ShapeDtypeStruct((rows, n_g * heads * hd), jnp.bfloat16),
        grid=(n_g, steps),
        in_specs=[
            pl.BlockSpec((f_step, 1, per, rows, rank), lambda g, s: (s, g, 0, 0, 0)),
            pl.BlockSpec((n_f, 1, f_step * per, cols, hd), lambda g, s: (0, g, s, 0, 0)),
        ],
        out_specs=pl.BlockSpec((rows, f_step * per * hd), lambda g, s: (0, g * steps + s)),
        compiler_params=pltpu.CompilerParams(vmem_limit_bytes=VMEM),
        cost_estimate=pl.CostEstimate(
            flops=2 * latent.size * hd,
            bytes_accessed=2 * (latent.size + values.size),
            transcendentals=0,
        ),
    )(latent, values)


def shards(n_fsdp, n_grp, q_up, k_up, v_up, queries, cache, positions):
    heads, hd, q_cols = q_up.shape
    own = heads // n_fsdp
    qk = jnp.concatenate([q_up, k_up], axis=-1)
    qk = qk.reshape(n_fsdp, own, hd, qk.shape[-1])
    values = lax.all_gather(jnp.swapaxes(v_up, 1, 2), ("fsdp", "grp"), axis=0)
    values = values.reshape(n_fsdp, n_grp, *values.shape[1:])
    q_abs = absorbed_queries(n_fsdp, n_grp, qk, queries, q_cols)
    row_queries = lax.all_to_all(q_abs, ("fsdp", "grp"), split_axis=0, concat_axis=0)
    latent = attend(row_queries, cache, positions, max(1, 16 // own))
    latent = latent.reshape(n_fsdp, n_grp, *latent.shape[1:])
    return project(latent, values, max(1, min(n_fsdp, 16 // own)))


def solution(mesh):
    placed = (
        P("grp", None, "fsdp"),
        P("grp", None, "fsdp"),
        P("grp", None, "fsdp"),
        P(("fsdp", "grp"), None),
        P(("fsdp", "grp"), None),
        P(("fsdp", "grp")),
    )
    return jax.shard_map(
        functools.partial(shards, mesh.shape["fsdp"], mesh.shape["grp"]),
        mesh=mesh,
        in_specs=placed,
        out_specs=P(("fsdp", "grp"), None),
        check_vma=False,
    )
```

```python
import functools

import jax
import jax.numpy as jnp
from jax import lax
from jax.experimental import pallas as pl
from jax.experimental.pallas import tpu as pltpu
from jax.sharding import PartitionSpec as P

score_scale = 192.0 ** (-0.5)
VMEM = 58 << 20


def body(n_fsdp, n_grp, q_cols, f_step, *refs):
    pos_ref, qk_ref, queries_ref, v_ref, cache_ref, out_ref = refs[:6]
    qk_all, rows_all, absorbed, q_send, q_recv, values, keys_all, latents = refs[6:14]
    (local_sem, qk_s, qk_r, grp_s, grp_r, far_s, far_r, pair_s, pair_r) = refs[14:23]
    (abs_s, abs_r, right_s, left_s, line_r) = refs[23:28]
    (b_s, a_s, ahead_s, aside_s, val_r, twin_s, twin_r) = refs[28:]
    f, g = lax.axis_index("fsdp"), lax.axis_index("grp")
    devices = n_fsdp * n_grp
    me = f * n_grp + g
    pairs = n_fsdp // 2
    n_a = pairs // 2
    chip, core = lax.div(f, 2), lax.rem(f, 2)
    a, b = lax.div(chip, 2), lax.rem(chip, 2)
    partner = chip * 2 + 1 - core
    b_peer = (a * 2 + 1 - b) * 2 + core
    own, rank = q_recv.shape[2], q_recv.shape[-1]
    rows = rows_all.shape[2]
    half_heads = values.shape[2] // 2
    hd = values.shape[-1]

    def send(src, dst, send_sem, recv_sem, to):
        return pltpu.make_async_remote_copy(
            src_ref=src,
            dst_ref=dst,
            send_sem=send_sem,
            recv_sem=recv_sem,
            device_id=to,
            device_id_type=pl.DeviceIdType.MESH,
        )

    barrier = pltpu.get_barrier_semaphore()

    @pl.loop(1, devices)
    def _(step):
        other = lax.rem(me + step, devices)
        pl.semaphore_signal(
            barrier,
            inc=1,
            device_id=(lax.div(other, n_grp), lax.rem(other, n_grp)),
            device_id_type=pl.DeviceIdType.MESH,
        )

    locals_ = [
        pltpu.make_async_copy(qk_ref.at[f], qk_all.at[f], local_sem.at[0]),
        pltpu.make_async_copy(queries_ref, rows_all.at[f, g], local_sem.at[1]),
        pltpu.make_async_copy(v_ref, values.at[f, g], local_sem.at[2]),
        pltpu.make_async_copy(cache_ref, keys_all, local_sem.at[3]),
    ]
    for copy in locals_:
        copy.start()
    pl.semaphore_wait(barrier, devices - 1)

    def grp_copy(peer, slot):
        return send(
            queries_ref, rows_all.at[f, slot], grp_s.at[peer], grp_r.at[slot], (f, peer)
        )

    def qk_copy(peer, slot):
        return send(qk_ref.at[peer], qk_all.at[slot], qk_s.at[peer], qk_r.at[slot], (peer, g))

    def far_copy(peer, slot):
        block = rows_all.at[slot]
        return send(block, block, far_s.at[peer], far_r.at[slot], (peer, g))

    def pair_copy(slot):
        block, k = rows_all.at[slot], lax.div(slot, 2)
        return send(block, block, pair_s.at[k], pair_r.at[k], (partner, g))

    def abs_copy(peer, slot):
        pf, pg = lax.div(peer, n_grp), lax.rem(peer, n_grp)
        sf, sg = lax.div(slot, n_grp), lax.rem(slot, n_grp)
        return send(q_send.at[pf, pg], q_recv.at[sf, sg], abs_s.at[peer], abs_r.at[slot], (pf, pg))

    def line_copy(src, slot, sems, to):
        return send(src, values.at[f, slot], sems.at[slot], line_r.at[slot], (f, to))

    def half(block, h):
        return values.at[block, :, pl.ds(h * half_heads, half_heads)]

    def val_copy(block, h, send_sem, to):
        return send(half(block, h), half(block, h), send_sem, val_r.at[block, h], (to, g))

    def twin_copy(block, h):
        k = lax.div(block, 2)
        return send(half(block, h), half(block, h), twin_s.at[k, h], twin_r.at[k, h], (partner, g))

    def a_peer(step):
        other = lax.rem(a + step, n_a)
        return other, (other * 2 + b) * 2 + core

    @pl.loop(1, n_grp)
    def _(step):
        grp_copy(lax.rem(g + step, n_grp), g).start()

    @pl.loop(1, n_fsdp)
    def _(step):
        qk_copy(lax.rem(f + step, n_fsdp), f).start()

    @pl.when(g < n_grp - 1)
    def _():
        line_copy(v_ref, g, right_s, g + 1).start()

    @pl.when(g > 0)
    def _():
        line_copy(v_ref, g, left_s, g - 1).start()

    locals_[1].wait()

    @pl.loop(1, n_grp)
    def _(step):
        other = lax.rem(g + step, n_grp)
        grp_copy(other, other).wait_recv()

    @pl.loop(1, pairs)
    def _(step):
        far_copy(lax.rem(chip + step, pairs) * 2 + core, f).start()

    pair_copy(f).start()

    @pl.loop(1, pairs)
    def _(step):
        other = lax.rem(chip + step, pairs) * 2 + core
        far_copy(other, other).wait_recv()
        pair_copy(other).start()

    def pass_on(k):
        @pl.when(g - k >= 0)
        def _():
            slot = g - k
            line_copy(values.at[f, slot], slot, right_s, g).wait_recv()

            @pl.when(g < n_grp - 1)
            def _():
                line_copy(values.at[f, slot], slot, right_s, g + 1).start()

        @pl.when(g + k < n_grp)
        def _():
            slot = g + k
            line_copy(values.at[f, slot], slot, left_s, g).wait_recv()

            @pl.when(g > 0)
            def _():
                line_copy(values.at[f, slot], slot, left_s, g - 1).start()

    for k in range(1, n_grp - 1):
        pass_on(k)

    locals_[0].wait()

    @pl.loop(1, n_fsdp)
    def _(step):
        other = lax.rem(f + step, n_fsdp)
        qk_copy(other, other).wait_recv()

    @pl.loop(0, own)
    def _(h):
        keys = jnp.concatenate([qk_all[s, h, :, q_cols:] for s in range(n_fsdp)], axis=-1)
        for s in range(n_fsdp):
            absorbed[h, s * q_cols : (s + 1) * q_cols, :] = lax.dot_general(
                qk_all[s, h, :, :q_cols],
                keys,
                (((0,), (0,)), ((), ())),
                preferred_element_type=jnp.float32,
            ).astype(jnp.bfloat16)

    @pl.loop(0, pairs)
    def _(step):
        pair_copy(step * 2 + 1 - core).wait_recv()

    @pl.loop(0, own)
    def _(h):
        block = rows_all[...].reshape(devices * rows, rows_all.shape[-1])
        q_abs = jnp.dot(block, absorbed[h], preferred_element_type=jnp.float32)
        q_send[:, :, h] = q_abs.astype(jnp.bfloat16).reshape(n_fsdp, n_grp, rows, rank)

    @pl.loop(1, devices)
    def _(step):
        abs_copy(lax.rem(me + step, devices), me).start()

    q_recv[f, g] = q_send[f, g]

    locals_[2].wait()
    pass_on(n_grp - 1)
    for h in range(2):
        val_copy(f, h, b_s.at[h], b_peer).start()
        twin_copy(f, h).start()

        @pl.loop(1, n_a)
        def _(step, h=h):
            other, peer = a_peer(step)
            val_copy(f, h, a_s.at[other, h], peer).start()

    locals_[3].wait()
    blocks = n_fsdp // f_step
    middle = (n_grp * blocks) // 2

    @pl.loop(0, n_grp * blocks)
    def _(step):
        sg = lax.rem(g + lax.div(step, blocks), n_grp)
        first = lax.rem(step, blocks) * f_step

        @pl.when(step == middle)
        def _():
            for h in range(2):
                val_copy(b_peer, h, b_s.at[h], b_peer).wait_recv()
                twin_copy(b_peer, h).start()

            @pl.loop(1, n_a)
            def _(hop):
                other, peer = a_peer(hop)
                val_copy(b_peer, 0, ahead_s.at[other], peer).start()

            @pl.loop(1, n_a)
            def _(hop):
                other, peer = a_peer(hop)
                for h in (1, 0):
                    val_copy(peer, h, a_s.at[other, h], peer).wait_recv()
                    twin_copy(peer, h).start()
                    if h == 1:
                        val_copy(peer, 1, aside_s.at[other], b_peer).start()

        @pl.loop(0, f_step)
        def _(j):
            src = (first + j) * n_grp + sg

            @pl.when(src != me)
            def _():
                abs_copy(src, src).wait_recv()

        q = q_recv[pl.ds(first, f_step), sg].reshape(f_step * own * rows, rank)
        entries = keys_all.shape[0]
        index = lax.broadcasted_iota(jnp.int32, (q.shape[0], entries), 1)
        scores = lax.dot_general(
            q, keys_all[...], (((1,), (1,)), ((), ())), preferred_element_type=jnp.float32
        )
        scores = jnp.where(index <= pos_ref[...], scores * score_scale, jnp.float32(-1e30))
        top = jnp.max(scores, axis=-1, keepdims=True)
        weights = jnp.exp(scores - top)
        total = jnp.sum(weights, axis=-1, keepdims=True)
        probs = (weights * (1.0 / total)).astype(jnp.bfloat16)
        latent = jnp.dot(probs, keys_all[...], preferred_element_type=jnp.float32)
        latents[pl.ds(first, f_step), sg] = latent.astype(jnp.bfloat16).reshape(
            f_step, own, rows, rank
        )

    @pl.loop(1, n_a)
    def _(hop):
        other, peer = a_peer(hop)
        diagonal = (other * 2 + 1 - b) * 2 + core
        for h in range(2):
            val_copy(diagonal, h, ahead_s.at[other], peer).wait_recv()
            twin_copy(diagonal, h).start()

    @pl.loop(0, pairs)
    def _(k):
        for h in range(2):
            twin_copy(k * 2 + 1 - core, h).wait_recv()

    heads = n_fsdp * own

    @pl.loop(0, devices)
    def _(step):
        sg, sf = lax.div(step, n_fsdp), lax.rem(step, n_fsdp)
        for i in range(own):
            h = sf * own + i
            column = pl.multiple_of((sg * heads + h) * hd, hd)
            out_ref[:, pl.ds(column, hd)] = jnp.dot(
                latents[sf, sg, i],
                values[:, sg, h].reshape(rank, hd),
                preferred_element_type=jnp.float32,
            ).astype(jnp.bfloat16)

    @pl.loop(1, n_grp)
    def _(step):
        grp_copy(lax.rem(g + step, n_grp), g).wait_send()

    @pl.loop(1, n_fsdp)
    def _(step):
        qk_copy(lax.rem(f + step, n_fsdp), f).wait_send()

    @pl.loop(1, pairs)
    def _(step):
        far_copy(lax.rem(chip + step, pairs) * 2 + core, f).wait_send()

    @pl.loop(0, pairs)
    def _(step):
        pair_copy(step * 2 + core).wait_send()
        for h in range(2):
            twin_copy(step * 2 + core, h).wait_send()

    @pl.loop(1, devices)
    def _(step):
        abs_copy(lax.rem(me + step, devices), me).wait_send()

    @pl.loop(0, n_grp)
    def _(slot):
        @pl.when(jnp.logical_and(slot <= g, g < n_grp - 1))
        def _():
            line_copy(values.at[f, slot], slot, right_s, g + 1).wait_send()

        @pl.when(jnp.logical_and(slot >= g, g > 0))
        def _():
            line_copy(values.at[f, slot], slot, left_s, g - 1).wait_send()

    for h in range(2):
        val_copy(f, h, b_s.at[h], b_peer).wait_send()

    @pl.loop(1, n_a)
    def _(hop):
        other, peer = a_peer(hop)
        for h in range(2):
            val_copy(f, h, a_s.at[other, h], peer).wait_send()
        val_copy(b_peer, 0, ahead_s.at[other], peer).wait_send()
        val_copy(peer, 1, aside_s.at[other], b_peer).wait_send()


def shards(n_fsdp, n_grp, q_up, k_up, v_up, queries, cache, positions):
    heads, hd, q_cols = q_up.shape
    own = heads // n_fsdp
    k_cols = k_up.shape[-1]
    rank = n_fsdp * k_cols
    rows, q_rank = queries.shape
    devices = n_fsdp * n_grp
    pairs = n_fsdp // 2
    n_a = pairs // 2
    f_step = max(1, min(n_fsdp, 16 // own))
    qk = jnp.concatenate([q_up, k_up], axis=-1).reshape(n_fsdp, own, hd, q_cols + k_cols)
    pos = jnp.tile(positions, f_step * own)[:, None]
    dma = pltpu.SemaphoreType.DMA
    bf16 = jnp.bfloat16
    anywhere = pl.BlockSpec(memory_space=pl.ANY)
    vmem = pl.BlockSpec(memory_space=pltpu.VMEM)
    exchange = (n_fsdp, n_grp, own, rows, rank)
    return pl.pallas_call(
        functools.partial(body, n_fsdp, n_grp, q_cols, f_step),
        out_shape=jax.ShapeDtypeStruct((rows, n_grp * heads * hd), bf16),
        in_specs=[vmem, anywhere, anywhere, anywhere, anywhere],
        out_specs=vmem,
        scratch_shapes=[
            pltpu.VMEM(qk.shape, bf16),
            pltpu.VMEM((n_fsdp, n_grp, rows, q_rank), bf16),
            pltpu.VMEM((own, q_rank, rank), bf16),
            pltpu.VMEM(exchange, bf16),
            pltpu.VMEM(exchange, bf16),
            pltpu.VMEM((n_fsdp, n_grp, heads, k_cols, hd), bf16),
            pltpu.VMEM(cache.shape, bf16),
            pltpu.VMEM(exchange, bf16),
            dma((4,)),
            dma((n_fsdp,)),
            dma((n_fsdp,)),
            dma((n_grp,)),
            dma((n_grp,)),
            dma((n_fsdp,)),
            dma((n_fsdp,)),
            dma((pairs,)),
            dma((pairs,)),
            dma((devices,)),
            dma((devices,)),
            dma((n_grp,)),
            dma((n_grp,)),
            dma((n_grp,)),
            dma((2,)),
            dma((n_a, 2)),
            dma((n_a,)),
            dma((n_a,)),
            dma((n_fsdp, 2)),
            dma((pairs, 2)),
            dma((pairs, 2)),
        ],
        compiler_params=pltpu.CompilerParams(
            vmem_limit_bytes=VMEM, collective_id=0, has_side_effects=True
        ),
    )(pos, qk, queries, jnp.swapaxes(v_up, 1, 2), cache)


def solution(mesh):
    placed = (
        P("grp", None, "fsdp"),
        P("grp", None, "fsdp"),
        P("grp", None, "fsdp"),
        P(("fsdp", "grp"), None),
        P(("fsdp", "grp"), None),
        P(("fsdp", "grp")),
    )
    return jax.shard_map(
        functools.partial(shards, mesh.shape["fsdp"], mesh.shape["grp"]),
        mesh=mesh,
        in_specs=placed,
        out_specs=P(("fsdp", "grp"), None),
        check_vma=False,
    )
```

```python
import functools

import jax
import jax.numpy as jnp
from jax import lax
from jax.experimental import pallas as pl
from jax.experimental.pallas import tpu as pltpu
from jax.sharding import PartitionSpec as P

score_scale = 192.0 ** (-0.5)
VMEM = 58 << 20


def body(n_fsdp, n_grp, q_cols, f_step, *refs):
    pos_ref, qk_ref, queries_ref, v_ref, cache_ref, out_ref = refs[:6]
    qk_all, rows_all, absorbed, q_send, q_recv, values, keys_all, latents = refs[6:14]
    (local_sem, qk_s, qk_r, grp_s, grp_r, far_s, far_r, pair_s, pair_r) = refs[14:23]
    (abs_s, abs_r, right_s, left_s, line_r) = refs[23:28]
    (b_s, a_s, ahead_s, aside_s, val_r, twin_s, twin_r) = refs[28:]
    f, g = lax.axis_index("fsdp"), lax.axis_index("grp")
    devices = n_fsdp * n_grp
    me = f * n_grp + g
    pairs = n_fsdp // 2
    n_a = pairs // 2
    chip, core = lax.div(f, 2), lax.rem(f, 2)
    a, b = lax.div(chip, 2), lax.rem(chip, 2)
    partner = chip * 2 + 1 - core
    b_peer = (a * 2 + 1 - b) * 2 + core
    own, rank = q_recv.shape[2], q_recv.shape[-1]
    rows = rows_all.shape[2]
    half_heads = values.shape[2] // 2
    hd = values.shape[-1]

    def send(src, dst, send_sem, recv_sem, to):
        return pltpu.make_async_remote_copy(
            src_ref=src,
            dst_ref=dst,
            send_sem=send_sem,
            recv_sem=recv_sem,
            device_id=to,
            device_id_type=pl.DeviceIdType.MESH,
        )

    barrier = pltpu.get_barrier_semaphore()

    @pl.loop(1, devices)
    def _(step):
        other = lax.rem(me + step, devices)
        pl.semaphore_signal(
            barrier,
            inc=1,
            device_id=(lax.div(other, n_grp), lax.rem(other, n_grp)),
            device_id_type=pl.DeviceIdType.MESH,
        )

    locals_ = [
        pltpu.make_async_copy(qk_ref.at[f], qk_all.at[f], local_sem.at[0]),
        pltpu.make_async_copy(queries_ref, rows_all.at[f, g], local_sem.at[1]),
        pltpu.make_async_copy(v_ref, values.at[f, g], local_sem.at[2]),
        pltpu.make_async_copy(cache_ref, keys_all, local_sem.at[3]),
    ]
    for copy in locals_:
        copy.start()
    pl.semaphore_wait(barrier, devices - 1)

    def grp_copy(peer, slot):
        return send(
            queries_ref, rows_all.at[f, slot], grp_s.at[peer], grp_r.at[slot], (f, peer)
        )

    def qk_copy(peer, slot):
        return send(qk_ref.at[peer], qk_all.at[slot], qk_s.at[peer], qk_r.at[slot], (peer, g))

    def far_copy(peer, slot):
        block = rows_all.at[slot]
        return send(block, block, far_s.at[peer], far_r.at[slot], (peer, g))

    def pair_copy(slot):
        block, k = rows_all.at[slot], lax.div(slot, 2)
        return send(block, block, pair_s.at[k], pair_r.at[k], (partner, g))

    def abs_copy(peer, slot):
        pf, pg = lax.div(peer, n_grp), lax.rem(peer, n_grp)
        sf, sg = lax.div(slot, n_grp), lax.rem(slot, n_grp)
        return send(q_send.at[pf, pg], q_recv.at[sf, sg], abs_s.at[peer], abs_r.at[slot], (pf, pg))

    def line_copy(src, slot, sems, to):
        return send(src, values.at[f, slot], sems.at[slot], line_r.at[slot], (f, to))

    def half(block, h):
        return values.at[block, :, pl.ds(h * half_heads, half_heads)]

    def val_copy(block, h, send_sem, to):
        return send(half(block, h), half(block, h), send_sem, val_r.at[block, h], (to, g))

    def twin_copy(block, h):
        k = lax.div(block, 2)
        return send(half(block, h), half(block, h), twin_s.at[k, h], twin_r.at[k, h], (partner, g))

    def a_peer(step):
        other = lax.rem(a + step, n_a)
        return other, (other * 2 + b) * 2 + core

    @pl.loop(1, n_grp)
    def _(step):
        grp_copy(lax.rem(g + step, n_grp), g).start()

    @pl.loop(1, n_fsdp)
    def _(step):
        qk_copy(lax.rem(f + step, n_fsdp), f).start()

    @pl.when(g < n_grp - 1)
    def _():
        line_copy(v_ref, g, right_s, g + 1).start()

    @pl.when(g > 0)
    def _():
        line_copy(v_ref, g, left_s, g - 1).start()

    locals_[1].wait()

    @pl.loop(1, n_grp)
    def _(step):
        other = lax.rem(g + step, n_grp)
        grp_copy(other, other).wait_recv()

    @pl.loop(1, pairs)
    def _(step):
        far_copy(lax.rem(chip + step, pairs) * 2 + core, f).start()

    pair_copy(f).start()

    @pl.loop(1, pairs)
    def _(step):
        other = lax.rem(chip + step, pairs) * 2 + core
        far_copy(other, other).wait_recv()
        pair_copy(other).start()

    def pass_on(k):
        @pl.when(g - k >= 0)
        def _():
            slot = g - k
            line_copy(values.at[f, slot], slot, right_s, g).wait_recv()

            @pl.when(g < n_grp - 1)
            def _():
                line_copy(values.at[f, slot], slot, right_s, g + 1).start()

        @pl.when(g + k < n_grp)
        def _():
            slot = g + k
            line_copy(values.at[f, slot], slot, left_s, g).wait_recv()

            @pl.when(g > 0)
            def _():
                line_copy(values.at[f, slot], slot, left_s, g - 1).start()

    for k in range(1, n_grp - 1):
        pass_on(k)

    locals_[0].wait()

    @pl.loop(1, n_fsdp)
    def _(step):
        other = lax.rem(f + step, n_fsdp)
        qk_copy(other, other).wait_recv()

    @pl.loop(0, own)
    def _(h):
        keys = jnp.concatenate([qk_all[s, h, :, q_cols:] for s in range(n_fsdp)], axis=-1)
        for s in range(n_fsdp):
            absorbed[h, s * q_cols : (s + 1) * q_cols, :] = lax.dot_general(
                qk_all[s, h, :, :q_cols],
                keys,
                (((0,), (0,)), ((), ())),
                preferred_element_type=jnp.float32,
            ).astype(jnp.bfloat16)

    @pl.loop(0, pairs)
    def _(step):
        pair_copy(step * 2 + 1 - core).wait_recv()

    @pl.loop(0, own)
    def _(h):
        block = rows_all[...].reshape(devices * rows, rows_all.shape[-1])
        q_abs = jnp.dot(block, absorbed[h], preferred_element_type=jnp.float32)
        q_send[:, :, h] = q_abs.astype(jnp.bfloat16).reshape(n_fsdp, n_grp, rows, rank)

    @pl.loop(1, devices)
    def _(step):
        abs_copy(lax.rem(me + step, devices), me).start()

    q_recv[f, g] = q_send[f, g]

    locals_[3].wait()
    blocks = n_fsdp // f_step
    middle = (n_grp * blocks) // 2

    @pl.loop(0, n_grp * blocks)
    def _(step):
        sg = lax.rem(g + lax.div(step, blocks), n_grp)
        first = lax.rem(step, blocks) * f_step

        @pl.when(step == blocks)
        def _():
            locals_[2].wait()
            pass_on(n_grp - 1)
            for h in range(2):
                val_copy(f, h, b_s.at[h], b_peer).start()
                twin_copy(f, h).start()

                @pl.loop(1, n_a)
                def _(step, h=h):
                    other, peer = a_peer(step)
                    val_copy(f, h, a_s.at[other, h], peer).start()

        @pl.when(step == middle)
        def _():
            for h in range(2):
                val_copy(b_peer, h, b_s.at[h], b_peer).wait_recv()
                twin_copy(b_peer, h).start()

            @pl.loop(1, n_a)
            def _(hop):
                other, peer = a_peer(hop)
                val_copy(b_peer, 0, ahead_s.at[other], peer).start()

            @pl.loop(1, n_a)
            def _(hop):
                other, peer = a_peer(hop)
                for h in (1, 0):
                    val_copy(peer, h, a_s.at[other, h], peer).wait_recv()
                    twin_copy(peer, h).start()
                    if h == 1:
                        val_copy(peer, 1, aside_s.at[other], b_peer).start()

        @pl.loop(0, f_step)
        def _(j):
            src = (first + j) * n_grp + sg

            @pl.when(src != me)
            def _():
                abs_copy(src, src).wait_recv()

        q = q_recv[pl.ds(first, f_step), sg].reshape(f_step * own * rows, rank)
        entries = keys_all.shape[0]
        index = lax.broadcasted_iota(jnp.int32, (q.shape[0], entries), 1)
        scores = lax.dot_general(
            q, keys_all[...], (((1,), (1,)), ((), ())), preferred_element_type=jnp.float32
        )
        scores = jnp.where(index <= pos_ref[...], scores * score_scale, jnp.float32(-1e30))
        top = jnp.max(scores, axis=-1, keepdims=True)
        weights = jnp.exp(scores - top)
        total = jnp.sum(weights, axis=-1, keepdims=True)
        probs = (weights * (1.0 / total)).astype(jnp.bfloat16)
        latent = jnp.dot(probs, keys_all[...], preferred_element_type=jnp.float32)
        latents[pl.ds(first, f_step), sg] = latent.astype(jnp.bfloat16).reshape(
            f_step, own, rows, rank
        )

    @pl.loop(1, n_a)
    def _(hop):
        other, peer = a_peer(hop)
        diagonal = (other * 2 + 1 - b) * 2 + core
        for h in range(2):
            val_copy(diagonal, h, ahead_s.at[other], peer).wait_recv()
            twin_copy(diagonal, h).start()

    @pl.loop(0, pairs)
    def _(k):
        for h in range(2):
            twin_copy(k * 2 + 1 - core, h).wait_recv()

    heads = n_fsdp * own

    @pl.loop(0, devices)
    def _(step):
        sg, sf = lax.div(step, n_fsdp), lax.rem(step, n_fsdp)
        for i in range(own):
            h = sf * own + i
            column = pl.multiple_of((sg * heads + h) * hd, hd)
            out_ref[:, pl.ds(column, hd)] = jnp.dot(
                latents[sf, sg, i],
                values[:, sg, h].reshape(rank, hd),
                preferred_element_type=jnp.float32,
            ).astype(jnp.bfloat16)

    @pl.loop(1, n_grp)
    def _(step):
        grp_copy(lax.rem(g + step, n_grp), g).wait_send()

    @pl.loop(1, n_fsdp)
    def _(step):
        qk_copy(lax.rem(f + step, n_fsdp), f).wait_send()

    @pl.loop(1, pairs)
    def _(step):
        far_copy(lax.rem(chip + step, pairs) * 2 + core, f).wait_send()

    @pl.loop(0, pairs)
    def _(step):
        pair_copy(step * 2 + core).wait_send()
        for h in range(2):
            twin_copy(step * 2 + core, h).wait_send()

    @pl.loop(1, devices)
    def _(step):
        abs_copy(lax.rem(me + step, devices), me).wait_send()

    @pl.loop(0, n_grp)
    def _(slot):
        @pl.when(jnp.logical_and(slot <= g, g < n_grp - 1))
        def _():
            line_copy(values.at[f, slot], slot, right_s, g + 1).wait_send()

        @pl.when(jnp.logical_and(slot >= g, g > 0))
        def _():
            line_copy(values.at[f, slot], slot, left_s, g - 1).wait_send()

    for h in range(2):
        val_copy(f, h, b_s.at[h], b_peer).wait_send()

    @pl.loop(1, n_a)
    def _(hop):
        other, peer = a_peer(hop)
        for h in range(2):
            val_copy(f, h, a_s.at[other, h], peer).wait_send()
        val_copy(b_peer, 0, ahead_s.at[other], peer).wait_send()
        val_copy(peer, 1, aside_s.at[other], b_peer).wait_send()


def shards(n_fsdp, n_grp, q_up, k_up, v_up, queries, cache, positions):
    heads, hd, q_cols = q_up.shape
    own = heads // n_fsdp
    k_cols = k_up.shape[-1]
    rank = n_fsdp * k_cols
    rows, q_rank = queries.shape
    devices = n_fsdp * n_grp
    pairs = n_fsdp // 2
    n_a = pairs // 2
    f_step = max(1, min(n_fsdp, 16 // own))
    qk = jnp.concatenate([q_up, k_up], axis=-1).reshape(n_fsdp, own, hd, q_cols + k_cols)
    pos = jnp.tile(positions, f_step * own)[:, None]
    dma = pltpu.SemaphoreType.DMA
    bf16 = jnp.bfloat16
    anywhere = pl.BlockSpec(memory_space=pl.ANY)
    vmem = pl.BlockSpec(memory_space=pltpu.VMEM)
    exchange = (n_fsdp, n_grp, own, rows, rank)
    return pl.pallas_call(
        functools.partial(body, n_fsdp, n_grp, q_cols, f_step),
        out_shape=jax.ShapeDtypeStruct((rows, n_grp * heads * hd), bf16),
        in_specs=[vmem, anywhere, anywhere, anywhere, anywhere],
        out_specs=vmem,
        scratch_shapes=[
            pltpu.VMEM(qk.shape, bf16),
            pltpu.VMEM((n_fsdp, n_grp, rows, q_rank), bf16),
            pltpu.VMEM((own, q_rank, rank), bf16),
            pltpu.VMEM(exchange, bf16),
            pltpu.VMEM(exchange, bf16),
            pltpu.VMEM((n_fsdp, n_grp, heads, k_cols, hd), bf16),
            pltpu.VMEM(cache.shape, bf16),
            pltpu.VMEM(exchange, bf16),
            dma((4,)),
            dma((n_fsdp,)),
            dma((n_fsdp,)),
            dma((n_grp,)),
            dma((n_grp,)),
            dma((n_fsdp,)),
            dma((n_fsdp,)),
            dma((pairs,)),
            dma((pairs,)),
            dma((devices,)),
            dma((devices,)),
            dma((n_grp,)),
            dma((n_grp,)),
            dma((n_grp,)),
            dma((2,)),
            dma((n_a, 2)),
            dma((n_a,)),
            dma((n_a,)),
            dma((n_fsdp, 2)),
            dma((pairs, 2)),
            dma((pairs, 2)),
        ],
        compiler_params=pltpu.CompilerParams(
            vmem_limit_bytes=VMEM, collective_id=0, has_side_effects=True
        ),
    )(pos, qk, queries, jnp.swapaxes(v_up, 1, 2), cache)


def solution(mesh):
    placed = (
        P("grp", None, "fsdp"),
        P("grp", None, "fsdp"),
        P("grp", None, "fsdp"),
        P(("fsdp", "grp"), None),
        P(("fsdp", "grp"), None),
        P(("fsdp", "grp")),
    )
    return jax.shard_map(
        functools.partial(shards, mesh.shape["fsdp"], mesh.shape["grp"]),
        mesh=mesh,
        in_specs=placed,
        out_specs=P(("fsdp", "grp"), None),
        check_vma=False,
    )
```

```python
import functools

import jax
import jax.numpy as jnp
from jax import lax
from jax.experimental import pallas as pl
from jax.experimental.pallas import tpu as pltpu
from jax.sharding import PartitionSpec as P

score_scale = 192.0 ** (-0.5)
VMEM = 58 << 20


def body(n_fsdp, n_grp, q_cols, f_step, *refs):
    pos_ref, qk_ref, queries_ref, v_ref, cache_ref, out_ref = refs[:6]
    qk_all, rows_all, absorbed, q_send, q_recv, values, keys_all, latents = refs[6:14]
    (local_sem, qk_s, qk_r, grp_s, grp_r, far_s, far_r, pair_s, pair_r) = refs[14:23]
    (abs_s, abs_r, right_s, left_s, line_r) = refs[23:28]
    (b_s, a_s, ahead_s, aside_s, val_r, twin_s, twin_r) = refs[28:]
    f, g = lax.axis_index("fsdp"), lax.axis_index("grp")
    devices = n_fsdp * n_grp
    me = f * n_grp + g
    pairs = n_fsdp // 2
    n_a = pairs // 2
    chip, core = lax.div(f, 2), lax.rem(f, 2)
    a, b = lax.div(chip, 2), lax.rem(chip, 2)
    partner = chip * 2 + 1 - core
    b_peer = (a * 2 + 1 - b) * 2 + core
    own, rank = q_recv.shape[2], q_recv.shape[-1]
    rows = rows_all.shape[2]
    half_heads = values.shape[2] // 2
    hd = values.shape[-1]

    def send(src, dst, send_sem, recv_sem, to):
        return pltpu.make_async_remote_copy(
            src_ref=src,
            dst_ref=dst,
            send_sem=send_sem,
            recv_sem=recv_sem,
            device_id=to,
            device_id_type=pl.DeviceIdType.MESH,
        )

    barrier = pltpu.get_barrier_semaphore()

    @pl.loop(1, devices)
    def _(step):
        other = lax.rem(me + step, devices)
        pl.semaphore_signal(
            barrier,
            inc=1,
            device_id=(lax.div(other, n_grp), lax.rem(other, n_grp)),
            device_id_type=pl.DeviceIdType.MESH,
        )

    locals_ = [
        pltpu.make_async_copy(qk_ref.at[f], qk_all.at[f], local_sem.at[0]),
        pltpu.make_async_copy(queries_ref, rows_all.at[f, g], local_sem.at[1]),
        pltpu.make_async_copy(v_ref, values.at[f, g], local_sem.at[2]),
        pltpu.make_async_copy(cache_ref, keys_all, local_sem.at[3]),
    ]
    for copy in locals_:
        copy.start()
    pl.semaphore_wait(barrier, devices - 1)

    def grp_copy(peer, slot):
        return send(
            queries_ref, rows_all.at[f, slot], grp_s.at[peer], grp_r.at[slot], (f, peer)
        )

    def qk_copy(peer, slot):
        return send(qk_ref.at[peer], qk_all.at[slot], qk_s.at[peer], qk_r.at[slot], (peer, g))

    def far_copy(peer, slot):
        block = rows_all.at[slot]
        return send(block, block, far_s.at[peer], far_r.at[slot], (peer, g))

    def pair_copy(slot):
        block, k = rows_all.at[slot], lax.div(slot, 2)
        return send(block, block, pair_s.at[k], pair_r.at[k], (partner, g))

    def abs_copy(peer, slot):
        pf, pg = lax.div(peer, n_grp), lax.rem(peer, n_grp)
        sf, sg = lax.div(slot, n_grp), lax.rem(slot, n_grp)
        return send(q_send.at[pf, pg], q_recv.at[sf, sg], abs_s.at[peer], abs_r.at[slot], (pf, pg))

    def line_copy(src, slot, sems, to):
        return send(src, values.at[f, slot], sems.at[slot], line_r.at[slot], (f, to))

    def half(block, h):
        return values.at[block, :, pl.ds(h * half_heads, half_heads)]

    def val_copy(block, h, send_sem, to):
        return send(half(block, h), half(block, h), send_sem, val_r.at[block, h], (to, g))

    def twin_copy(block, h):
        k = lax.div(block, 2)
        return send(half(block, h), half(block, h), twin_s.at[k, h], twin_r.at[k, h], (partner, g))

    def a_peer(step):
        other = lax.rem(a + step, n_a)
        return other, (other * 2 + b) * 2 + core

    @pl.loop(1, n_grp)
    def _(step):
        grp_copy(lax.rem(g + step, n_grp), g).start()

    @pl.loop(1, n_fsdp)
    def _(step):
        qk_copy(lax.rem(f + step, n_fsdp), f).start()

    @pl.when(g < n_grp - 1)
    def _():
        line_copy(v_ref, g, right_s, g + 1).start()

    @pl.when(g > 0)
    def _():
        line_copy(v_ref, g, left_s, g - 1).start()

    locals_[1].wait()

    @pl.loop(1, n_grp)
    def _(step):
        other = lax.rem(g + step, n_grp)
        grp_copy(other, other).wait_recv()

    @pl.loop(1, pairs)
    def _(step):
        far_copy(lax.rem(chip + step, pairs) * 2 + core, f).start()

    pair_copy(f).start()

    @pl.loop(1, pairs)
    def _(step):
        other = lax.rem(chip + step, pairs) * 2 + core
        far_copy(other, other).wait_recv()
        pair_copy(other).start()

    def pass_on(k):
        @pl.when(g - k >= 0)
        def _():
            slot = g - k
            line_copy(values.at[f, slot], slot, right_s, g).wait_recv()

            @pl.when(g < n_grp - 1)
            def _():
                line_copy(values.at[f, slot], slot, right_s, g + 1).start()

        @pl.when(g + k < n_grp)
        def _():
            slot = g + k
            line_copy(values.at[f, slot], slot, left_s, g).wait_recv()

            @pl.when(g > 0)
            def _():
                line_copy(values.at[f, slot], slot, left_s, g - 1).start()

    for k in range(1, n_grp - 1):
        pass_on(k)

    locals_[0].wait()

    @pl.loop(1, n_fsdp)
    def _(step):
        other = lax.rem(f + step, n_fsdp)
        qk_copy(other, other).wait_recv()

    @pl.loop(0, own)
    def _(h):
        keys = jnp.concatenate([qk_all[s, h, :, q_cols:] for s in range(n_fsdp)], axis=-1)
        for s in range(n_fsdp):
            absorbed[h, s * q_cols : (s + 1) * q_cols, :] = lax.dot_general(
                qk_all[s, h, :, :q_cols],
                keys,
                (((0,), (0,)), ((), ())),
                preferred_element_type=jnp.float32,
            ).astype(jnp.bfloat16)

    @pl.loop(0, pairs)
    def _(step):
        pair_copy(step * 2 + 1 - core).wait_recv()

    @pl.loop(0, own)
    def _(h):
        block = rows_all[...].reshape(devices * rows, rows_all.shape[-1])
        q_abs = jnp.dot(block, absorbed[h], preferred_element_type=jnp.float32)
        q_send[:, :, h] = q_abs.astype(jnp.bfloat16).reshape(n_fsdp, n_grp, rows, rank)

    @pl.loop(1, devices)
    def _(step):
        abs_copy(lax.rem(me + step, devices), me).start()

    q_recv[f, g] = q_send[f, g]

    locals_[2].wait()
    pass_on(n_grp - 1)
    for h in range(2):
        val_copy(f, h, b_s.at[h], b_peer).start()

        @pl.loop(1, n_a)
        def _(step, h=1 - h):
            other, peer = a_peer(step)
            val_copy(f, h, a_s.at[other, h], peer).start()

    for h in range(2):
        twin_copy(f, h).start()

    locals_[3].wait()
    blocks = n_fsdp // f_step
    middle = (n_grp * blocks) // 2

    @pl.loop(0, n_grp * blocks)
    def _(step):
        sg = lax.rem(g + lax.div(step, blocks), n_grp)
        first = lax.rem(step, blocks) * f_step

        @pl.when(step == middle)
        def _():
            for h in range(2):
                val_copy(b_peer, h, b_s.at[h], b_peer).wait_recv()
                twin_copy(b_peer, h).start()

            @pl.loop(1, n_a)
            def _(hop):
                other, peer = a_peer(hop)
                val_copy(b_peer, 0, ahead_s.at[other], peer).start()

            @pl.loop(1, n_a)
            def _(hop):
                other, peer = a_peer(hop)
                for h in (1, 0):
                    val_copy(peer, h, a_s.at[other, h], peer).wait_recv()
                    twin_copy(peer, h).start()
                    if h == 1:
                        val_copy(peer, 1, aside_s.at[other], b_peer).start()

        @pl.loop(0, f_step)
        def _(j):
            src = (first + j) * n_grp + sg

            @pl.when(src != me)
            def _():
                abs_copy(src, src).wait_recv()

        q = q_recv[pl.ds(first, f_step), sg].reshape(f_step * own * rows, rank)
        entries = keys_all.shape[0]
        index = lax.broadcasted_iota(jnp.int32, (q.shape[0], entries), 1)
        scores = lax.dot_general(
            q, keys_all[...], (((1,), (1,)), ((), ())), preferred_element_type=jnp.float32
        )
        scores = jnp.where(index <= pos_ref[...], scores * score_scale, jnp.float32(-1e30))
        top = jnp.max(scores, axis=-1, keepdims=True)
        weights = jnp.exp(scores - top)
        total = jnp.sum(weights, axis=-1, keepdims=True)
        probs = (weights * (1.0 / total)).astype(jnp.bfloat16)
        latent = jnp.dot(probs, keys_all[...], preferred_element_type=jnp.float32)
        latents[pl.ds(first, f_step), sg] = latent.astype(jnp.bfloat16).reshape(
            f_step, own, rows, rank
        )

    @pl.loop(1, n_a)
    def _(hop):
        other, peer = a_peer(hop)
        diagonal = (other * 2 + 1 - b) * 2 + core
        for h in range(2):
            val_copy(diagonal, h, ahead_s.at[other], peer).wait_recv()
            twin_copy(diagonal, h).start()

    @pl.loop(0, pairs)
    def _(k):
        for h in range(2):
            twin_copy(k * 2 + 1 - core, h).wait_recv()

    heads = n_fsdp * own

    @pl.loop(0, devices)
    def _(step):
        sg, sf = lax.div(step, n_fsdp), lax.rem(step, n_fsdp)
        for i in range(own):
            h = sf * own + i
            column = pl.multiple_of((sg * heads + h) * hd, hd)
            out_ref[:, pl.ds(column, hd)] = jnp.dot(
                latents[sf, sg, i],
                values[:, sg, h].reshape(rank, hd),
                preferred_element_type=jnp.float32,
            ).astype(jnp.bfloat16)

    @pl.loop(1, n_grp)
    def _(step):
        grp_copy(lax.rem(g + step, n_grp), g).wait_send()

    @pl.loop(1, n_fsdp)
    def _(step):
        qk_copy(lax.rem(f + step, n_fsdp), f).wait_send()

    @pl.loop(1, pairs)
    def _(step):
        far_copy(lax.rem(chip + step, pairs) * 2 + core, f).wait_send()

    @pl.loop(0, pairs)
    def _(step):
        pair_copy(step * 2 + core).wait_send()
        for h in range(2):
            twin_copy(step * 2 + core, h).wait_send()

    @pl.loop(1, devices)
    def _(step):
        abs_copy(lax.rem(me + step, devices), me).wait_send()

    @pl.loop(0, n_grp)
    def _(slot):
        @pl.when(jnp.logical_and(slot <= g, g < n_grp - 1))
        def _():
            line_copy(values.at[f, slot], slot, right_s, g + 1).wait_send()

        @pl.when(jnp.logical_and(slot >= g, g > 0))
        def _():
            line_copy(values.at[f, slot], slot, left_s, g - 1).wait_send()

    for h in range(2):
        val_copy(f, h, b_s.at[h], b_peer).wait_send()

    @pl.loop(1, n_a)
    def _(hop):
        other, peer = a_peer(hop)
        for h in range(2):
            val_copy(f, h, a_s.at[other, h], peer).wait_send()
        val_copy(b_peer, 0, ahead_s.at[other], peer).wait_send()
        val_copy(peer, 1, aside_s.at[other], b_peer).wait_send()


def shards(n_fsdp, n_grp, q_up, k_up, v_up, queries, cache, positions):
    heads, hd, q_cols = q_up.shape
    own = heads // n_fsdp
    k_cols = k_up.shape[-1]
    rank = n_fsdp * k_cols
    rows, q_rank = queries.shape
    devices = n_fsdp * n_grp
    pairs = n_fsdp // 2
    n_a = pairs // 2
    f_step = max(1, min(n_fsdp, 16 // own))
    qk = jnp.concatenate([q_up, k_up], axis=-1).reshape(n_fsdp, own, hd, q_cols + k_cols)
    pos = jnp.tile(positions, f_step * own)[:, None]
    dma = pltpu.SemaphoreType.DMA
    bf16 = jnp.bfloat16
    anywhere = pl.BlockSpec(memory_space=pl.ANY)
    vmem = pl.BlockSpec(memory_space=pltpu.VMEM)
    exchange = (n_fsdp, n_grp, own, rows, rank)
    return pl.pallas_call(
        functools.partial(body, n_fsdp, n_grp, q_cols, f_step),
        out_shape=jax.ShapeDtypeStruct((rows, n_grp * heads * hd), bf16),
        in_specs=[vmem, anywhere, anywhere, anywhere, anywhere],
        out_specs=vmem,
        scratch_shapes=[
            pltpu.VMEM(qk.shape, bf16),
            pltpu.VMEM((n_fsdp, n_grp, rows, q_rank), bf16),
            pltpu.VMEM((own, q_rank, rank), bf16),
            pltpu.VMEM(exchange, bf16),
            pltpu.VMEM(exchange, bf16),
            pltpu.VMEM((n_fsdp, n_grp, heads, k_cols, hd), bf16),
            pltpu.VMEM(cache.shape, bf16),
            pltpu.VMEM(exchange, bf16),
            dma((4,)),
            dma((n_fsdp,)),
            dma((n_fsdp,)),
            dma((n_grp,)),
            dma((n_grp,)),
            dma((n_fsdp,)),
            dma((n_fsdp,)),
            dma((pairs,)),
            dma((pairs,)),
            dma((devices,)),
            dma((devices,)),
            dma((n_grp,)),
            dma((n_grp,)),
            dma((n_grp,)),
            dma((2,)),
            dma((n_a, 2)),
            dma((n_a,)),
            dma((n_a,)),
            dma((n_fsdp, 2)),
            dma((pairs, 2)),
            dma((pairs, 2)),
        ],
        compiler_params=pltpu.CompilerParams(
            vmem_limit_bytes=VMEM, collective_id=0, has_side_effects=True
        ),
    )(pos, qk, queries, jnp.swapaxes(v_up, 1, 2), cache)


def solution(mesh):
    placed = (
        P("grp", None, "fsdp"),
        P("grp", None, "fsdp"),
        P("grp", None, "fsdp"),
        P(("fsdp", "grp"), None),
        P(("fsdp", "grp"), None),
        P(("fsdp", "grp")),
    )
    return jax.shard_map(
        functools.partial(shards, mesh.shape["fsdp"], mesh.shape["grp"]),
        mesh=mesh,
        in_specs=placed,
        out_specs=P(("fsdp", "grp"), None),
        check_vma=False,
    )
```
